32 devices in a mesh: tp: 2 (over x), wide: 16 (over z, y, core).
Axes of the slice: x: 2, y: 2, z: 4, core: 2. Of those that a mesh axis runs over, the one named last changes fastest.
Arguments:
- token_keys: bfloat16 [2048, 28672], P('tp', 'wide'), may hold values from -6 to 6
- resid_grad: bfloat16 [2048, 8192], P('wide', 'tp'), may hold values from -6 to 6
- kv_grad: bfloat16 [2048, 2048], P('wide', 'tp'), may hold values from -6 to 6
- kv_weight: bfloat16 [8192, 2048], P('wide', 'tp'), may hold values from -0.125 to 0.125
- editor_in: bfloat16 [8192, 1920], P('tp'), may hold values from -0.0625 to 0.0625
- editor_bias: float32 [1920], replicated, may hold values from -3 to 3
- editor_gain: float32 [8192], P('tp'), may hold values from 0.5 to 1.5
- editor_out: bfloat16 [1920, 8192], P(None, 'tp'), may hold values from -0.125 to 0.125
- prompt_len: int32 [32], replicated, may hold values from 1 to 63
Outputs:
- weight_update: bfloat16 [28672, 8192], P('wide', 'tp')
The draws below stay inside these ranges and needn't reach their ends.
All inputs are finite; a program needn't handle non-finite values.
Results may differ from the reference program's by a relative error of at most 0.0055.
Values may be sent and summed in bfloat16 or wider, within the bound.
A program may use at most 128 MiB of HBM per device.

```python
import jax
import jax.numpy as jnp
from jax import lax

D = 8192
FF = 28672
KV = 2048
RANK = 1920
LEN = 64
TOKENS = 2048
EXAMPLES = 32


def with_ends(entries, key, smallest, largest):
    longest = entries.shape.index(max(entries.shape))
    spots = []
    for shift in (0, 1):
        where = [jax.random.randint(jax.random.fold_in(key, axis), (), 0, length) for axis, length in enumerate(entries.shape)]
        where[longest] = (where[longest] + shift) % entries.shape[longest]
        spots.append(tuple(where))
    return entries.at[spots[0]].set(smallest).at[spots[1]].set(largest)


def level_of(key, dims, pieces, low, largest):
    def one(axis_at, blocks):
        draws = jax.random.uniform(jax.random.fold_in(jax.random.fold_in(key, 6), axis_at), (blocks,), jnp.float32, low / len(pieces), largest / len(pieces))
        return jnp.repeat(jnp.exp(draws), dims[axis_at] // blocks).reshape((-1,) + (1,) * (len(dims) - axis_at - 1))

    gain = one(*pieces[0])
    for cut in pieces[1:]:
        gain = gain * one(*cut)
    return gain


def noise(key, dims, spread, limit, split=(), held_as=jnp.bfloat16):
    factor_of = level_of(key, dims, split, -0.22, 0.18) if split else 1.0
    result = jax.random.normal(key, dims, jnp.float32) * spread * factor_of
    return jnp.minimum(jnp.maximum(result, -limit), limit).astype(held_as)


def setup_inputs(seed: int = 0) -> dict:
    key_of = jax.random.split(jax.random.key(seed), 10)
    token_keys = noise(key_of[0], (TOKENS, FF), 1.0, 6.0, ((0, 2), (1, 16)))
    resid_grad = noise(key_of[1], (TOKENS, D), 1.0, 6.0, ((0, 16), (1, 2)))
    kv_grad = noise(key_of[2], (TOKENS, KV), 1.0, 6.0, ((0, 16), (1, 2)))
    kv_weight = noise(key_of[3], (D, KV), KV ** -0.5, 0.125, ((0, 16), (1, 2)))
    editor_in = noise(key_of[4], (D, RANK), D ** -0.5, 0.0625, ((0, 2),))
    editor_bias = noise(key_of[5], (RANK,), 0.5, 3.0, (), jnp.float32)
    editor_gain = jnp.clip(1.0 + 0.1 * jax.random.normal(key_of[6], (D,), jnp.float32), 0.5, 1.5)
    editor_out = noise(key_of[7], (RANK, D), RANK ** -0.5, 0.125, ((1, 2),))
    prompt_len = with_ends(jax.random.randint(key_of[8], (EXAMPLES,), 1, LEN), jax.random.fold_in(key_of[8], 1), 1, LEN - 1).astype(jnp.int32)
    return {"token_keys": token_keys, "resid_grad": resid_grad, "kv_grad": kv_grad, "kv_weight": kv_weight, "editor_in": editor_in, "editor_bias": editor_bias, "editor_gain": editor_gain, "editor_out": editor_out, "prompt_len": prompt_len}


def reference(token_keys, resid_grad, kv_grad, kv_weight, editor_in, editor_bias, editor_gain, editor_out, prompt_len):
    kv_term = lax.dot_general(kv_grad, kv_weight, (((1,), (1,)), ((), ())), preferred_element_type=jnp.float32)
    gradient = resid_grad.astype(jnp.float32) + kv_term
    inv_rms = lax.rsqrt(lax.optimization_barrier(jnp.mean(gradient * gradient, axis=1, keepdims=True)) + 1e-06)
    scaled = (gradient * editor_gain.astype(jnp.float32)).astype(jnp.bfloat16)
    projected = jnp.dot(scaled, editor_in, preferred_element_type=jnp.float32)
    hidden = jnp.maximum(projected * inv_rms + editor_bias.astype(jnp.float32), 0.0).astype(jnp.bfloat16)
    starts = jnp.repeat(prompt_len.astype(jnp.int32), LEN, total_repeat_length=TOKENS)
    position = jnp.arange(TOKENS, dtype=jnp.int32) % LEN
    keep_mask = (position >= starts).astype(jnp.float32)
    edited = ((gradient + jnp.dot(hidden, editor_out, preferred_element_type=jnp.float32)) * keep_mask[:, None]).astype(jnp.bfloat16)
    edit_count = jnp.sum(LEN - prompt_len).astype(jnp.float32)
    summed = lax.dot_general(token_keys, edited, (((0,), (0,)), ((), ())), preferred_element_type=jnp.float32)
    return (summed * lax.rsqrt(edit_count)).astype(jnp.bfloat16)
```

```python
import functools

import jax
import jax.numpy as jnp
from jax import lax
from jax.experimental import pallas as pl
from jax.experimental.pallas import tpu as pltpu
from jax.sharding import PartitionSpec as P

LEN = 64
EPSILON = 1e-06
MESH = pl.DeviceIdType.MESH
F32, BF16 = jnp.float32, jnp.bfloat16
MIB = 1 << 20


def gather_blocks(piece, chunks, outer, inner, sems, consume):
    line_send, peer_send, pair_send, recv = sems
    me = lax.axis_index("wide")
    a, b, c = me // (2 * inner), (me // 2) % inner, me % 2

    def ident(a1, b1, c1):
        return (a1 * inner + b1) * 2 + c1

    def copy(owner, q, send, target):
        ref = piece(owner, q)
        return pltpu.make_async_remote_copy(
            src_ref=ref, dst_ref=ref, send_sem=send, recv_sem=recv.at[owner, q],
            device_id={"wide": target}, device_id_type=MESH,
        )

    def arrived(owner, q):
        copy(owner, q, pair_send.at[owner, q], ident(a, b, 1 - c)).wait_recv()

    def line_copies(dist, sign, q, do):
        a1 = a + sign * dist
        owner = ident(a1, b, c)
        for way in (-1, 1):
            onward = a + way
            goes = (onward >= 0) & (onward < outer) & ((dist == 0) | (way == -sign))

            @pl.when(goes)
            def _():
                do(copy(owner, q, line_send.at[owner, q, (way + 1) // 2], ident(onward, b, c)))

        for k in range(1, inner):
            do(copy(owner, q, peer_send.at[owner, q, k - 1], ident(a, (b + k) % inner, c)))
        do(copy(owner, q, pair_send.at[owner, q], ident(a, b, 1 - c)))

    def on_line(i, todo):
        for sign in (-1, 1):
            dist, q = i // chunks, i % chunks
            a1 = a + sign * dist
            here = (i >= 0) & (dist < outer) & (a1 >= 0) & (a1 < outer)
            if sign == -1:
                here = here & (dist > 0)

            @pl.when(here)
            def _():
                todo(dist, sign, q, a1)

    def step(i, carry):
        def first(dist, sign, q, a1):
            owner = ident(a1, b, c)

            @pl.when(dist > 0)
            def _():
                arrived(owner, q)

            line_copies(dist, sign, q, lambda made: made.start())
            consume(owner, q)

        on_line(i, first)

        def second(dist, sign, q, a1):
            for k in range(1, inner):
                owner = ident(a1, (b + k) % inner, c)
                arrived(owner, q)
                copy(owner, q, pair_send.at[owner, q], ident(a, b, 1 - c)).start()
                consume(owner, q)

        on_line(i - chunks, second)

        def third(dist, sign, q, a1):
            for k in range(inner):
                owner = ident(a1, (b + k) % inner, 1 - c)
                arrived(owner, q)
                consume(owner, q)

        on_line(i - 2 * chunks, third)
        return carry

    lax.fori_loop(0, (outer + 2) * chunks, step, 0)

    def drain():
        def finish(i, carry):
            def sent(dist, sign, q, a1):
                line_copies(dist, sign, q, lambda made: made.wait_send())
                for k in range(1, inner):
                    owner = ident(a1, (b + k) % inner, c)
                    copy(owner, q, pair_send.at[owner, q], ident(a, b, 1 - c)).wait_send()

            on_line(i, sent)
            return carry

        lax.fori_loop(0, outer * chunks, finish, 0)

    return drain


def edit_kernel(
    tp, n, outer, inner, chunks, width,
    keys, resid, kv_grad, kv_weight, editor_in, bias, gain, editor_out, prompt_len,
    keys_all, edited_all,
    kv_all, product, parts, grad, in_held, out_held, hid, hid_send, hid_recv, sq_send, sq_recv, edited,
    local, line1, peer1, pair1, recv1, line2, peer2, pair2, recv2,
    part_send, part_recv, hid_ssem, hid_rsem, sq_ssem, sq_rsem, key_ssem, key_rsem,
):
    t, w = lax.axis_index("tp"), lax.axis_index("wide")
    rows = resid.shape[0]
    columns = resid.shape[1]
    tile = kv_weight.shape[0]
    per = columns // tile
    key_rows = keys.shape[0]
    owner_t, slot = w // per, w % per

    in_copy = pltpu.make_async_copy(editor_in, in_held, local.at[0])
    out_copy = pltpu.make_async_copy(editor_out, out_held, local.at[1])
    own_keys = pltpu.make_async_copy(keys, keys_all.at[pl.ds(t * key_rows, key_rows)], local.at[2])
    in_copy.start()
    out_copy.start()

    barrier = pltpu.get_barrier_semaphore()

    def greet(i, carry):
        @pl.when(i != t * n + w)
        def _():
            pl.semaphore_signal(barrier, inc=1, device_id={"tp": i // n, "wide": i % n}, device_id_type=MESH)

        return carry

    lax.fori_loop(0, tp * n, greet, 0)
    kv_all[w] = kv_grad[...]
    pl.semaphore_wait(barrier, tp * n - 1)

    def part_copy(owner):
        return pltpu.make_async_remote_copy(
            src_ref=product.at[owner], dst_ref=parts.at[t, slot],
            send_sem=part_send.at[owner], recv_sem=part_recv.at[t, slot],
            device_id={"tp": owner_t, "wide": owner}, device_id_type=MESH,
        )

    def multiply(owner, q):
        term = lax.dot_general(
            kv_all[owner], kv_weight[...], (((1,), (1,)), ((), ())), preferred_element_type=F32
        ).astype(BF16)
        stays = (owner_t == t) & (owner == w)

        @pl.when(stays)
        def _():
            parts[t, slot] = term

        @pl.when(jnp.logical_not(stays))
        def _():
            product[owner] = term
            part_copy(owner).start()

    drain1 = gather_blocks(
        lambda owner, q: kv_all.at[owner], 1, outer, inner, (line1, peer1, pair1, recv1), multiply
    )
    in_copy.wait()

    hid[...] = jnp.zeros_like(hid)
    sq_send[...] = jnp.zeros_like(sq_send)

    def take(k, carry):
        for source in range(tp):
            @pl.when(jnp.logical_not((source == t) & (t * per + k == w)))
            def _():
                pltpu.make_async_remote_copy(
                    src_ref=product.at[0], dst_ref=parts.at[source, k],
                    send_sem=part_send.at[0], recv_sem=part_recv.at[source, k],
                    device_id={"tp": t, "wide": w}, device_id_type=MESH,
                ).wait_recv()

        at = pl.ds(pl.multiple_of(k * tile, tile), tile)
        term = parts[0, k].astype(F32)
        for source in range(1, tp):
            term = term + parts[source, k].astype(F32)
        block = term + resid[:, at].astype(F32)
        grad[:, at] = block
        sq_send[...] += jnp.broadcast_to(jnp.sum(block * block, axis=1, keepdims=True), sq_send.shape)
        scaled = (block * gain[:, at]).astype(BF16)
        hid[...] += jnp.dot(scaled, in_held[at, :], preferred_element_type=F32)
        return carry

    lax.fori_loop(0, per, take, 0)
    hid_send[...] = hid[...].astype(BF16)

    def hid_copies(k):
        to = (t + k) % tp
        return (
            pltpu.make_async_remote_copy(
                src_ref=hid_send, dst_ref=hid_recv.at[k - 1], send_sem=hid_ssem.at[k - 1],
                recv_sem=hid_rsem.at[k - 1], device_id={"tp": to}, device_id_type=MESH),
            pltpu.make_async_remote_copy(
                src_ref=sq_send, dst_ref=sq_recv.at[k - 1], send_sem=sq_ssem.at[k - 1],
                recv_sem=sq_rsem.at[k - 1], device_id={"tp": to}, device_id_type=MESH),
        )

    def key_copy(k):
        return pltpu.make_async_remote_copy(
            src_ref=keys, dst_ref=keys_all.at[pl.ds(t * key_rows, key_rows)], send_sem=key_ssem.at[k - 1],
            recv_sem=key_rsem.at[k - 1], device_id={"tp": (t + k) % tp}, device_id_type=MESH)

    for k in range(1, tp):
        for made in hid_copies(k):
            made.start()
    own_keys.start()
    for k in range(1, tp):
        key_copy(k).start()
    out_copy.wait()
    squares = sq_send[:, :1]
    for k in range(1, tp):
        for made in hid_copies(k):
            made.wait_recv()
        hid[...] += hid_recv[k - 1].astype(F32)
        squares = squares + sq_recv[k - 1][:, :1]
    inv_rms = lax.rsqrt(squares / width + EPSILON)
    hid_send_free = [made for k in range(1, tp) for made in hid_copies(k)]
    for made in hid_send_free:
        made.wait_send()
    hid_send[...] = jnp.maximum(hid[...] * inv_rms + bias[...], 0.0).astype(BF16)

    examples = rows // LEN
    masks = []
    for e in range(examples):
        start = prompt_len[w * examples + e]
        masks.append((lax.broadcasted_iota(jnp.int32, (LEN, 1), 0) >= start).astype(F32))
    keep = jnp.concatenate(masks, axis=0)

    def edit(k, carry):
        at = pl.ds(pl.multiple_of(k * tile, tile), tile)
        total = grad[:, at] + jnp.dot(hid_send[...], out_held[:, at], preferred_element_type=F32)
        edited[:, at] = (total * keep).astype(BF16)
        return carry

    lax.fori_loop(0, per, edit, 0)
    own_edited = pltpu.make_async_copy(
        edited, edited_all.at[pl.ds(pl.multiple_of(w * rows, rows), rows)], local.at[3])
    own_edited.start()
    own_edited.wait()

    part = rows // chunks
    drain2 = gather_blocks(
        lambda owner, q: edited_all.at[pl.ds(pl.multiple_of(owner * rows + q * part, part), part)],
        chunks, outer, inner, (line2, peer2, pair2, recv2), lambda owner, q: None,
    )

    drain1()

    def sent(i, carry):
        @pl.when(jnp.logical_not((owner_t == t) & (i == w)))
        def _():
            part_copy(i).wait_send()

        return carry

    lax.fori_loop(0, n, sent, 0)
    drain2()
    own_keys.wait()
    for k in range(1, tp):
        key_copy(k).wait_send()
        source = (t + tp - k) % tp
        pltpu.make_async_remote_copy(
            src_ref=keys, dst_ref=keys_all.at[pl.ds(source * key_rows, key_rows)], send_sem=key_ssem.at[k - 1],
            recv_sem=key_rsem.at[k - 1], device_id={"tp": source}, device_id_type=MESH).wait_recv()


def update_kernel(prompt_len, keys, edited, out):
    def count(i, total):
        return total + (LEN - prompt_len[i])

    edit_count = lax.fori_loop(0, prompt_len.shape[0], count, 0)
    scale = lax.rsqrt(jnp.full((1, 1), edit_count, jnp.int32).astype(F32))
    summed = lax.dot_general(keys[...], edited[...], (((0,), (0,)), ((), ())), preferred_element_type=F32)
    out[...] = (summed * scale).astype(BF16)


def per_device(
    tp, n, token_keys, resid_grad, kv_grad, kv_weight, editor_in, editor_bias, editor_gain, editor_out, prompt_len
):
    outer = 4 if n % 8 == 0 else 1
    inner = n // (2 * outer)
    chunks = 2
    rows, columns = resid_grad.shape
    tile, kv_local = kv_weight.shape
    per = columns // tile
    rank = editor_in.shape[1]
    key_rows, key_columns = token_keys.shape
    vmem = pl.BlockSpec(memory_space=pltpu.VMEM)
    hbm = pl.BlockSpec(memory_space=pl.ANY)
    smem = pl.BlockSpec(memory_space=pltpu.SMEM)
    dma = pltpu.SemaphoreType.DMA
    peers = max(inner - 1, 1)
    others = max(tp - 1, 1)
    keys_all, edited_all = pl.pallas_call(
        functools.partial(edit_kernel, tp, n, outer, inner, chunks, columns * tp),
        out_shape=(
            jax.ShapeDtypeStruct((tp * key_rows, key_columns), BF16),
            jax.ShapeDtypeStruct((n * rows, columns), BF16),
        ),
        in_specs=[hbm, vmem, vmem, vmem, hbm, vmem, vmem, hbm, smem],
        out_specs=(hbm, hbm),
        scratch_shapes=[
            pltpu.VMEM((n, rows, kv_local), BF16),
            pltpu.VMEM((n, rows, tile), BF16),
            pltpu.VMEM((tp, per, rows, tile), BF16),
            pltpu.VMEM((rows, columns), F32),
            pltpu.VMEM(editor_in.shape, BF16),
            pltpu.VMEM(editor_out.shape, BF16),
            pltpu.VMEM((rows, rank), F32),
            pltpu.VMEM((rows, rank), BF16),
            pltpu.VMEM((others, rows, rank), BF16),
            pltpu.VMEM((rows, 128), F32),
            pltpu.VMEM((others, rows, 128), F32),
            pltpu.VMEM((rows, columns), BF16),
            dma((4,)),
            dma((n, 1, 2)), dma((n, 1, peers)), dma((n, 1)), dma((n, 1)),
            dma((n, chunks, 2)), dma((n, chunks, peers)), dma((n, chunks)), dma((n, chunks)),
            dma((n,)), dma((tp, per)),
            dma((others,)), dma((others,)), dma((others,)), dma((others,)), dma((others,)), dma((others,)),
        ],
        compiler_params=pltpu.CompilerParams(
            collective_id=0, has_side_effects=True, vmem_limit_bytes=60 * MIB
        ),
    )(
        token_keys, resid_grad, kv_grad, kv_weight, editor_in, editor_bias.reshape(1, -1),
        editor_gain.reshape(1, -1), editor_out, prompt_len,
    )
    block = min(columns, 512)
    tokens = keys_all.shape[0]
    return pl.pallas_call(
        update_kernel,
        grid=(columns // block,),
        out_shape=jax.ShapeDtypeStruct((key_columns, columns), BF16),
        in_specs=[
            smem,
            pl.BlockSpec((tokens, key_columns), lambda i: (0, 0)),
            pl.BlockSpec((tokens, block), lambda i: (0, i)),
        ],
        out_specs=pl.BlockSpec((key_columns, block), lambda i: (0, i)),
        compiler_params=pltpu.CompilerParams(vmem_limit_bytes=60 * MIB),
    )(prompt_len, keys_all, edited_all)


def solution(mesh):
    in_specs = (
        P("tp", "wide"),
        P("wide", "tp"),
        P("wide", "tp"),
        P("wide", "tp"),
        P("tp", None),
        P(),
        P("tp"),
        P(None, "tp"),
        P(),
    )
    out_specs = P("wide", "tp")
    return jax.shard_map(
        functools.partial(per_device, mesh.shape["tp"], mesh.shape["wide"]),
        mesh=mesh, in_specs=in_specs, out_specs=out_specs, check_vma=False,
    )
```

```python
import functools

import jax
import jax.numpy as jnp
from jax import lax
from jax.experimental import pallas as pl
from jax.experimental.pallas import tpu as pltpu
from jax.sharding import PartitionSpec as P

LEN = 64
EPSILON = 1e-06
MESH = pl.DeviceIdType.MESH
F32, BF16 = jnp.float32, jnp.bfloat16
MIB = 1 << 20


def gather_blocks(piece, chunks, outer, inner, sems, consume):
    line_send, peer_send, pair_send, recv = sems
    me = lax.axis_index("wide")
    a, b, c = me // (2 * inner), (me // 2) % inner, me % 2

    def ident(a1, b1, c1):
        return (a1 * inner + b1) * 2 + c1

    def copy(owner, q, send, target):
        ref = piece(owner, q)
        return pltpu.make_async_remote_copy(
            src_ref=ref, dst_ref=ref, send_sem=send, recv_sem=recv.at[owner, q],
            device_id={"wide": target}, device_id_type=MESH,
        )

    def arrived(owner, q):
        copy(owner, q, pair_send.at[owner, q], ident(a, b, 1 - c)).wait_recv()

    def line_copies(dist, sign, q, do):
        a1 = a + sign * dist
        owner = ident(a1, b, c)
        for way in (-1, 1):
            onward = a + way
            goes = (onward >= 0) & (onward < outer) & ((dist == 0) | (way == -sign))

            @pl.when(goes)
            def _():
                do(copy(owner, q, line_send.at[owner, q, (way + 1) // 2], ident(onward, b, c)))

        for k in range(1, inner):
            do(copy(owner, q, peer_send.at[owner, q, k - 1], ident(a, (b + k) % inner, c)))
        do(copy(owner, q, pair_send.at[owner, q], ident(a, b, 1 - c)))

    def on_line(i, todo):
        for sign in (-1, 1):
            dist, q = i // chunks, i % chunks
            a1 = a + sign * dist
            here = (i >= 0) & (dist < outer) & (a1 >= 0) & (a1 < outer)
            if sign == -1:
                here = here & (dist > 0)

            @pl.when(here)
            def _():
                todo(dist, sign, q, a1)

    def step(i, carry):
        def first(dist, sign, q, a1):
            owner = ident(a1, b, c)

            @pl.when(dist > 0)
            def _():
                arrived(owner, q)

            line_copies(dist, sign, q, lambda made: made.start())
            consume(owner, q)

        on_line(i, first)

        def second(dist, sign, q, a1):
            for k in range(1, inner):
                owner = ident(a1, (b + k) % inner, c)
                arrived(owner, q)
                copy(owner, q, pair_send.at[owner, q], ident(a, b, 1 - c)).start()
                consume(owner, q)

        on_line(i - chunks, second)

        def third(dist, sign, q, a1):
            for k in range(inner):
                owner = ident(a1, (b + k) % inner, 1 - c)
                arrived(owner, q)
                consume(owner, q)

        on_line(i - 2 * chunks, third)
        return carry

    lax.fori_loop(0, (outer + 2) * chunks, step, 0)

    def drain():
        def finish(i, carry):
            def sent(dist, sign, q, a1):
                line_copies(dist, sign, q, lambda made: made.wait_send())
                for k in range(1, inner):
                    owner = ident(a1, (b + k) % inner, c)
                    copy(owner, q, pair_send.at[owner, q], ident(a, b, 1 - c)).wait_send()

            on_line(i, sent)
            return carry

        lax.fori_loop(0, outer * chunks, finish, 0)

    return drain


def edit_kernel(
    tp, n, outer, inner, chunks, width,
    keys, resid, kv_grad, kv_weight, editor_in, bias, gain, editor_out, prompt_len,
    keys_all, edited_all,
    kv_all, product, parts, grad, in_held, out_held, hid, hid_send, hid_recv, sq_send, sq_recv, edited, kv_turned,
    local, line1, peer1, pair1, recv1, line2, peer2, pair2, recv2,
    part_send, part_recv, hid_ssem, hid_rsem, sq_ssem, sq_rsem, key_ssem, key_rsem,
):
    t, w = lax.axis_index("tp"), lax.axis_index("wide")
    rows = resid.shape[0]
    columns = resid.shape[1]
    tile = kv_weight.shape[0]
    per = columns // tile
    key_rows = keys.shape[0]
    owner_t, slot = w // per, w % per

    in_copy = pltpu.make_async_copy(editor_in, in_held, local.at[0])
    out_copy = pltpu.make_async_copy(editor_out, out_held, local.at[1])
    own_keys = pltpu.make_async_copy(keys, keys_all.at[pl.ds(t * key_rows, key_rows)], local.at[2])
    in_copy.start()
    out_copy.start()
    own_keys.start()

    barrier = pltpu.get_barrier_semaphore()

    def greet(i, carry):
        @pl.when(i != t * n + w)
        def _():
            pl.semaphore_signal(barrier, inc=1, device_id={"tp": i // n, "wide": i % n}, device_id_type=MESH)

        return carry

    lax.fori_loop(0, tp * n, greet, 0)
    kv_all[w] = kv_grad[...]
    kv_turned[...] = kv_weight[...].T
    pl.semaphore_wait(barrier, tp * n - 1)

    def part_copy(owner):
        return pltpu.make_async_remote_copy(
            src_ref=product.at[owner], dst_ref=parts.at[t, slot],
            send_sem=part_send.at[owner], recv_sem=part_recv.at[t, slot],
            device_id={"tp": owner_t, "wide": owner}, device_id_type=MESH,
        )

    def multiply(owner, q):
        term = lax.dot_general(
            kv_all[owner], kv_turned[...], (((1,), (0,)), ((), ())), preferred_element_type=F32
        ).astype(BF16)
        stays = (owner_t == t) & (owner == w)

        @pl.when(stays)
        def _():
            parts[t, slot] = term

        @pl.when(jnp.logical_not(stays))
        def _():
            product[owner] = term
            part_copy(owner).start()

    drain1 = gather_blocks(
        lambda owner, q: kv_all.at[owner], 1, outer, inner, (line1, peer1, pair1, recv1), multiply
    )
    in_copy.wait()

    hid[...] = jnp.zeros_like(hid)
    sq_send[...] = jnp.zeros_like(sq_send)

    def take(k, carry):
        for source in range(tp):
            @pl.when(jnp.logical_not((source == t) & (t * per + k == w)))
            def _():
                pltpu.make_async_remote_copy(
                    src_ref=product.at[0], dst_ref=parts.at[source, k],
                    send_sem=part_send.at[0], recv_sem=part_recv.at[source, k],
                    device_id={"tp": t, "wide": w}, device_id_type=MESH,
                ).wait_recv()

        at = pl.ds(pl.multiple_of(k * tile, tile), tile)
        term = parts[0, k].astype(F32)
        for source in range(1, tp):
            term = term + parts[source, k].astype(F32)
        block = term + resid[:, at].astype(F32)
        grad[:, at] = block
        sq_send[...] += jnp.broadcast_to(jnp.sum(block * block, axis=1, keepdims=True), sq_send.shape)
        scaled = (block * gain[:, at]).astype(BF16)
        hid[...] += jnp.dot(scaled, in_held[at, :], preferred_element_type=F32)
        return carry

    lax.fori_loop(0, per, take, 0)
    hid_send[...] = hid[...].astype(BF16)

    def hid_copies(k):
        to = (t + k) % tp
        return (
            pltpu.make_async_remote_copy(
                src_ref=hid_send, dst_ref=hid_recv.at[k - 1], send_sem=hid_ssem.at[k - 1],
                recv_sem=hid_rsem.at[k - 1], device_id={"tp": to}, device_id_type=MESH),
            pltpu.make_async_remote_copy(
                src_ref=sq_send, dst_ref=sq_recv.at[k - 1], send_sem=sq_ssem.at[k - 1],
                recv_sem=sq_rsem.at[k - 1], device_id={"tp": to}, device_id_type=MESH),
        )

    def key_copy(k):
        return pltpu.make_async_remote_copy(
            src_ref=keys, dst_ref=keys_all.at[pl.ds(t * key_rows, key_rows)], send_sem=key_ssem.at[k - 1],
            recv_sem=key_rsem.at[k - 1], device_id={"tp": (t + k) % tp}, device_id_type=MESH)

    for k in range(1, tp):
        for made in hid_copies(k):
            made.start()
    for k in range(1, tp):
        key_copy(k).start()
    out_copy.wait()
    squares = sq_send[:, :1]
    for k in range(1, tp):
        for made in hid_copies(k):
            made.wait_recv()
        hid[...] += hid_recv[k - 1].astype(F32)
        squares = squares + sq_recv[k - 1][:, :1]
    inv_rms = lax.rsqrt(squares / width + EPSILON)
    hid_send_free = [made for k in range(1, tp) for made in hid_copies(k)]
    for made in hid_send_free:
        made.wait_send()
    hid_send[...] = jnp.maximum(hid[...] * inv_rms + bias[...], 0.0).astype(BF16)

    examples = rows // LEN
    masks = []
    for e in range(examples):
        start = prompt_len[w * examples + e]
        masks.append((lax.broadcasted_iota(jnp.int32, (LEN, 1), 0) >= start).astype(F32))
    keep = jnp.concatenate(masks, axis=0)

    def edit(k, carry):
        at = pl.ds(pl.multiple_of(k * tile, tile), tile)
        total = grad[:, at] + jnp.dot(hid_send[...], out_held[:, at], preferred_element_type=F32)
        edited[:, at] = (total * keep).astype(BF16)
        return carry

    lax.fori_loop(0, per, edit, 0)
    own_edited = pltpu.make_async_copy(
        edited, edited_all.at[pl.ds(pl.multiple_of(w * rows, rows), rows)], local.at[3])
    own_edited.start()
    own_edited.wait()

    part = rows // chunks
    drain2 = gather_blocks(
        lambda owner, q: edited_all.at[pl.ds(pl.multiple_of(owner * rows + q * part, part), part)],
        chunks, outer, inner, (line2, peer2, pair2, recv2), lambda owner, q: None,
    )

    drain1()

    def sent(i, carry):
        @pl.when(jnp.logical_not((owner_t == t) & (i == w)))
        def _():
            part_copy(i).wait_send()

        return carry

    lax.fori_loop(0, n, sent, 0)
    drain2()
    own_keys.wait()
    for k in range(1, tp):
        key_copy(k).wait_send()
        source = (t + tp - k) % tp
        pltpu.make_async_remote_copy(
            src_ref=keys, dst_ref=keys_all.at[pl.ds(source * key_rows, key_rows)], send_sem=key_ssem.at[k - 1],
            recv_sem=key_rsem.at[k - 1], device_id={"tp": source}, device_id_type=MESH).wait_recv()


def update_kernel(prompt_len, keys, edited, out):
    def count(i, total):
        return total + (LEN - prompt_len[i])

    edit_count = lax.fori_loop(0, prompt_len.shape[0], count, 0)
    scale = lax.rsqrt(jnp.full((1, 1), edit_count, jnp.int32).astype(F32))
    summed = lax.dot_general(keys[...], edited[...], (((0,), (0,)), ((), ())), preferred_element_type=F32)
    out[...] = (summed * scale).astype(BF16)


def per_device(
    tp, n, token_keys, resid_grad, kv_grad, kv_weight, editor_in, editor_bias, editor_gain, editor_out, prompt_len
):
    outer = 4 if n % 8 == 0 else 1
    inner = n // (2 * outer)
    chunks = 2
    rows, columns = resid_grad.shape
    tile, kv_local = kv_weight.shape
    per = columns // tile
    rank = editor_in.shape[1]
    key_rows, key_columns = token_keys.shape
    vmem = pl.BlockSpec(memory_space=pltpu.VMEM)
    hbm = pl.BlockSpec(memory_space=pl.ANY)
    smem = pl.BlockSpec(memory_space=pltpu.SMEM)
    dma = pltpu.SemaphoreType.DMA
    peers = max(inner - 1, 1)
    others = max(tp - 1, 1)
    keys_all, edited_all = pl.pallas_call(
        functools.partial(edit_kernel, tp, n, outer, inner, chunks, columns * tp),
        out_shape=(
            jax.ShapeDtypeStruct((tp * key_rows, key_columns), BF16),
            jax.ShapeDtypeStruct((n * rows, columns), BF16),
        ),
        in_specs=[hbm, vmem, vmem, vmem, hbm, vmem, vmem, hbm, smem],
        out_specs=(hbm, hbm),
        scratch_shapes=[
            pltpu.VMEM((n, rows, kv_local), BF16),
            pltpu.VMEM((n, rows, tile), BF16),
            pltpu.VMEM((tp, per, rows, tile), BF16),
            pltpu.VMEM((rows, columns), F32),
            pltpu.VMEM(editor_in.shape, BF16),
            pltpu.VMEM(editor_out.shape, BF16),
            pltpu.VMEM((rows, rank), F32),
            pltpu.VMEM((rows, rank), BF16),
            pltpu.VMEM((others, rows, rank), BF16),
            pltpu.VMEM((rows, 128), F32),
            pltpu.VMEM((others, rows, 128), F32),
            pltpu.VMEM((rows, columns), BF16),
            pltpu.VMEM((kv_local, tile), BF16),
            dma((4,)),
            dma((n, 1, 2)), dma((n, 1, peers)), dma((n, 1)), dma((n, 1)),
            dma((n, chunks, 2)), dma((n, chunks, peers)), dma((n, chunks)), dma((n, chunks)),
            dma((n,)), dma((tp, per)),
            dma((others,)), dma((others,)), dma((others,)), dma((others,)), dma((others,)), dma((others,)),
        ],
        compiler_params=pltpu.CompilerParams(
            collective_id=0, has_side_effects=True, vmem_limit_bytes=60 * MIB
        ),
    )(
        token_keys, resid_grad, kv_grad, kv_weight, editor_in, editor_bias.reshape(1, -1),
        editor_gain.reshape(1, -1), editor_out, prompt_len,
    )
    block = min(columns, 1024)
    tokens = keys_all.shape[0]
    return pl.pallas_call(
        update_kernel,
        grid=(columns // block,),
        out_shape=jax.ShapeDtypeStruct((key_columns, columns), BF16),
        in_specs=[
            smem,
            pl.BlockSpec((tokens, key_columns), lambda i: (0, 0)),
            pl.BlockSpec((tokens, block), lambda i: (0, i)),
        ],
        out_specs=pl.BlockSpec((key_columns, block), lambda i: (0, i)),
        compiler_params=pltpu.CompilerParams(vmem_limit_bytes=60 * MIB),
    )(prompt_len, keys_all, edited_all)


def solution(mesh):
    in_specs = (
        P("tp", "wide"),
        P("wide", "tp"),
        P("wide", "tp"),
        P("wide", "tp"),
        P("tp", None),
        P(),
        P("tp"),
        P(None, "tp"),
        P(),
    )
    out_specs = P("wide", "tp")
    return jax.shard_map(
        functools.partial(per_device, mesh.shape["tp"], mesh.shape["wide"]),
        mesh=mesh, in_specs=in_specs, out_specs=out_specs, check_vma=False,
    )
```

```python
import functools

import jax
import jax.numpy as jnp
from jax import lax
from jax.experimental import pallas as pl
from jax.experimental.pallas import tpu as pltpu
from jax.sharding import PartitionSpec as P

LEN = 64
EPSILON = 1e-06
MESH = pl.DeviceIdType.MESH
F32, BF16 = jnp.float32, jnp.bfloat16
MIB = 1 << 20


def gather_blocks(piece, chunks, outer, inner, sems, consume):
    line_send, peer_send, pair_send, recv = sems
    me = lax.axis_index("wide")
    a, b, c = me // (2 * inner), (me // 2) % inner, me % 2

    def ident(a1, b1, c1):
        return (a1 * inner + b1) * 2 + c1

    def copy(owner, q, send, target):
        ref = piece(owner, q)
        return pltpu.make_async_remote_copy(
            src_ref=ref, dst_ref=ref, send_sem=send, recv_sem=recv.at[owner, q],
            device_id={"wide": target}, device_id_type=MESH,
        )

    def arrived(owner, q):
        copy(owner, q, pair_send.at[owner, q], ident(a, b, 1 - c)).wait_recv()

    def line_copies(dist, sign, q, do):
        a1 = a + sign * dist
        owner = ident(a1, b, c)
        for way in (-1, 1):
            onward = a + way
            goes = (onward >= 0) & (onward < outer) & ((dist == 0) | (way == -sign))

            @pl.when(goes)
            def _():
                do(copy(owner, q, line_send.at[owner, q, (way + 1) // 2], ident(onward, b, c)))

        for k in range(1, inner):
            do(copy(owner, q, peer_send.at[owner, q, k - 1], ident(a, (b + k) % inner, c)))
        do(copy(owner, q, pair_send.at[owner, q], ident(a, b, 1 - c)))

    def on_line(i, todo):
        for sign in (-1, 1):
            dist, q = i // chunks, i % chunks
            a1 = a + sign * dist
            here = (i >= 0) & (dist < outer) & (a1 >= 0) & (a1 < outer)
            if sign == -1:
                here = here & (dist > 0)

            @pl.when(here)
            def _():
                todo(dist, sign, q, a1)

    def step(i, carry):
        def first(dist, sign, q, a1):
            owner = ident(a1, b, c)

            @pl.when(dist > 0)
            def _():
                arrived(owner, q)

            line_copies(dist, sign, q, lambda made: made.start())
            consume(owner, q)

        on_line(i, first)

        def second(dist, sign, q, a1):
            for k in range(1, inner):
                owner = ident(a1, (b + k) % inner, c)
                arrived(owner, q)
                copy(owner, q, pair_send.at[owner, q], ident(a, b, 1 - c)).start()
                consume(owner, q)

        on_line(i - chunks, second)

        def third(dist, sign, q, a1):
            for k in range(inner):
                owner = ident(a1, (b + k) % inner, 1 - c)
                arrived(owner, q)
                consume(owner, q)

        on_line(i - 2 * chunks, third)
        return carry

    lax.fori_loop(0, (outer + 2) * chunks, step, 0)

    def drain():
        def finish(i, carry):
            def sent(dist, sign, q, a1):
                line_copies(dist, sign, q, lambda made: made.wait_send())
                for k in range(1, inner):
                    owner = ident(a1, (b + k) % inner, c)
                    copy(owner, q, pair_send.at[owner, q], ident(a, b, 1 - c)).wait_send()

            on_line(i, sent)
            return carry

        lax.fori_loop(0, outer * chunks, finish, 0)

    return drain


def edit_kernel(
    tp, n, outer, inner, chunks, width,
    keys, resid, kv_grad, kv_weight, editor_in, bias, gain, editor_out, prompt_len,
    keys_all, edited_all,
    kv_all, product, parts, grad, in_held, out_held, hid, hid_send, hid_recv, sq_send, sq_recv, edited, kv_turned,
    local, line1, peer1, pair1, recv1, line2, peer2, pair2, recv2,
    part_send, part_recv, hid_ssem, hid_rsem, sq_ssem, sq_rsem, key_ssem, key_rsem,
):
    t, w = lax.axis_index("tp"), lax.axis_index("wide")
    rows = resid.shape[0]
    columns = resid.shape[1]
    tile = kv_weight.shape[0]
    per = columns // tile
    key_rows = keys.shape[0]
    owner_t, slot = w // per, w % per

    in_copy = pltpu.make_async_copy(editor_in, in_held, local.at[0])
    out_copy = pltpu.make_async_copy(editor_out, out_held, local.at[1])
    own_keys = pltpu.make_async_copy(keys, keys_all.at[pl.ds(t * key_rows, key_rows)], local.at[2])
    in_copy.start()
    out_copy.start()
    own_keys.start()

    barrier = pltpu.get_barrier_semaphore()

    def greet(i, carry):
        @pl.when(i != t * n + w)
        def _():
            pl.semaphore_signal(barrier, inc=1, device_id={"tp": i // n, "wide": i % n}, device_id_type=MESH)

        return carry

    lax.fori_loop(0, tp * n, greet, 0)
    kv_all[w] = kv_grad[...]
    kv_turned[...] = kv_weight[...].T
    pl.semaphore_wait(barrier, tp * n - 1)

    def part_copy(owner):
        return pltpu.make_async_remote_copy(
            src_ref=product.at[owner], dst_ref=parts.at[t, slot],
            send_sem=part_send.at[owner], recv_sem=part_recv.at[t, slot],
            device_id={"tp": owner_t, "wide": owner}, device_id_type=MESH,
        )

    def multiply(owner, q):
        term = lax.dot_general(
            kv_all[owner], kv_turned[...], (((1,), (0,)), ((), ())), preferred_element_type=F32
        ).astype(BF16)
        stays = (owner_t == t) & (owner == w)

        @pl.when(stays)
        def _():
            parts[t, slot] = term

        @pl.when(jnp.logical_not(stays))
        def _():
            product[owner] = term
            part_copy(owner).start()

    drain1 = gather_blocks(
        lambda owner, q: kv_all.at[owner, pl.ds(pl.multiple_of(q * (rows // chunks), rows // chunks), rows // chunks)],
        chunks, outer, inner, (line1, peer1, pair1, recv1),
        lambda owner, q: pl.when(q == chunks - 1)(lambda: multiply(owner, q)),
    )
    in_copy.wait()

    hid[...] = jnp.zeros_like(hid)
    sq_send[...] = jnp.zeros_like(sq_send)

    def take(k, carry):
        for source in range(tp):
            @pl.when(jnp.logical_not((source == t) & (t * per + k == w)))
            def _():
                pltpu.make_async_remote_copy(
                    src_ref=product.at[0], dst_ref=parts.at[source, k],
                    send_sem=part_send.at[0], recv_sem=part_recv.at[source, k],
                    device_id={"tp": t, "wide": w}, device_id_type=MESH,
                ).wait_recv()

        at = pl.ds(pl.multiple_of(k * tile, tile), tile)
        term = parts[0, k].astype(F32)
        for source in range(1, tp):
            term = term + parts[source, k].astype(F32)
        block = term + resid[:, at].astype(F32)
        grad[:, at] = block
        sq_send[...] += jnp.broadcast_to(jnp.sum(block * block, axis=1, keepdims=True), sq_send.shape)
        scaled = (block * gain[:, at]).astype(BF16)
        hid[...] += jnp.dot(scaled, in_held[at, :], preferred_element_type=F32)
        return carry

    lax.fori_loop(0, per, take, 0)
    hid_send[...] = hid[...].astype(BF16)

    def hid_copies(k):
        to = (t + k) % tp
        return (
            pltpu.make_async_remote_copy(
                src_ref=hid_send, dst_ref=hid_recv.at[k - 1], send_sem=hid_ssem.at[k - 1],
                recv_sem=hid_rsem.at[k - 1], device_id={"tp": to}, device_id_type=MESH),
            pltpu.make_async_remote_copy(
                src_ref=sq_send, dst_ref=sq_recv.at[k - 1], send_sem=sq_ssem.at[k - 1],
                recv_sem=sq_rsem.at[k - 1], device_id={"tp": to}, device_id_type=MESH),
        )

    def key_copy(k):
        return pltpu.make_async_remote_copy(
            src_ref=keys, dst_ref=keys_all.at[pl.ds(t * key_rows, key_rows)], send_sem=key_ssem.at[k - 1],
            recv_sem=key_rsem.at[k - 1], device_id={"tp": (t + k) % tp}, device_id_type=MESH)

    for k in range(1, tp):
        for made in hid_copies(k):
            made.start()
    for k in range(1, tp):
        key_copy(k).start()
    out_copy.wait()
    squares = sq_send[:, :1]
    for k in range(1, tp):
        for made in hid_copies(k):
            made.wait_recv()
        hid[...] += hid_recv[k - 1].astype(F32)
        squares = squares + sq_recv[k - 1][:, :1]
    inv_rms = lax.rsqrt(squares / width + EPSILON)
    hid_send_free = [made for k in range(1, tp) for made in hid_copies(k)]
    for made in hid_send_free:
        made.wait_send()
    hid_send[...] = jnp.maximum(hid[...] * inv_rms + bias[...], 0.0).astype(BF16)

    examples = rows // LEN
    masks = []
    for e in range(examples):
        start = prompt_len[w * examples + e]
        masks.append((lax.broadcasted_iota(jnp.int32, (LEN, 1), 0) >= start).astype(F32))
    keep = jnp.concatenate(masks, axis=0)

    def edit(k, carry):
        at = pl.ds(pl.multiple_of(k * tile, tile), tile)
        total = grad[:, at] + jnp.dot(hid_send[...], out_held[:, at], preferred_element_type=F32)
        edited[:, at] = (total * keep).astype(BF16)
        return carry

    lax.fori_loop(0, per, edit, 0)
    own_edited = pltpu.make_async_copy(
        edited, edited_all.at[pl.ds(pl.multiple_of(w * rows, rows), rows)], local.at[3])
    own_edited.start()
    own_edited.wait()

    part = rows // chunks
    drain2 = gather_blocks(
        lambda owner, q: edited_all.at[pl.ds(pl.multiple_of(owner * rows + q * part, part), part)],
        chunks, outer, inner, (line2, peer2, pair2, recv2), lambda owner, q: None,
    )

    drain1()

    def sent(i, carry):
        @pl.when(jnp.logical_not((owner_t == t) & (i == w)))
        def _():
            part_copy(i).wait_send()

        return carry

    lax.fori_loop(0, n, sent, 0)
    drain2()
    own_keys.wait()
    for k in range(1, tp):
        key_copy(k).wait_send()
        source = (t + tp - k) % tp
        pltpu.make_async_remote_copy(
            src_ref=keys, dst_ref=keys_all.at[pl.ds(source * key_rows, key_rows)], send_sem=key_ssem.at[k - 1],
            recv_sem=key_rsem.at[k - 1], device_id={"tp": source}, device_id_type=MESH).wait_recv()


def update_kernel(prompt_len, keys, edited, out):
    def count(i, total):
        return total + (LEN - prompt_len[i])

    edit_count = lax.fori_loop(0, prompt_len.shape[0], count, 0)
    scale = lax.rsqrt(jnp.full((1, 1), edit_count, jnp.int32).astype(F32))
    summed = lax.dot_general(keys[...], edited[...], (((0,), (0,)), ((), ())), preferred_element_type=F32)
    out[...] = (summed * scale).astype(BF16)


def per_device(
    tp, n, token_keys, resid_grad, kv_grad, kv_weight, editor_in, editor_bias, editor_gain, editor_out, prompt_len
):
    outer = 4 if n % 8 == 0 else 1
    inner = n // (2 * outer)
    chunks = 2
    rows, columns = resid_grad.shape
    tile, kv_local = kv_weight.shape
    per = columns // tile
    rank = editor_in.shape[1]
    key_rows, key_columns = token_keys.shape
    vmem = pl.BlockSpec(memory_space=pltpu.VMEM)
    hbm = pl.BlockSpec(memory_space=pl.ANY)
    smem = pl.BlockSpec(memory_space=pltpu.SMEM)
    dma = pltpu.SemaphoreType.DMA
    peers = max(inner - 1, 1)
    others = max(tp - 1, 1)
    keys_all, edited_all = pl.pallas_call(
        functools.partial(edit_kernel, tp, n, outer, inner, chunks, columns * tp),
        out_shape=(
            jax.ShapeDtypeStruct((tp * key_rows, key_columns), BF16),
            jax.ShapeDtypeStruct((n * rows, columns), BF16),
        ),
        in_specs=[hbm, vmem, vmem, vmem, hbm, vmem, vmem, hbm, smem],
        out_specs=(hbm, hbm),
        scratch_shapes=[
            pltpu.VMEM((n, rows, kv_local), BF16),
            pltpu.VMEM((n, rows, tile), BF16),
            pltpu.VMEM((tp, per, rows, tile), BF16),
            pltpu.VMEM((rows, columns), F32),
            pltpu.VMEM(editor_in.shape, BF16),
            pltpu.VMEM(editor_out.shape, BF16),
            pltpu.VMEM((rows, rank), F32),
            pltpu.VMEM((rows, rank), BF16),
            pltpu.VMEM((others, rows, rank), BF16),
            pltpu.VMEM((rows, 128), F32),
            pltpu.VMEM((others, rows, 128), F32),
            pltpu.VMEM((rows, columns), BF16),
            pltpu.VMEM((kv_local, tile), BF16),
            dma((4,)),
            dma((n, chunks, 2)), dma((n, chunks, peers)), dma((n, chunks)), dma((n, chunks)),
            dma((n, chunks, 2)), dma((n, chunks, peers)), dma((n, chunks)), dma((n, chunks)),
            dma((n,)), dma((tp, per)),
            dma((others,)), dma((others,)), dma((others,)), dma((others,)), dma((others,)), dma((others,)),
        ],
        compiler_params=pltpu.CompilerParams(
            collective_id=0, has_side_effects=True, vmem_limit_bytes=60 * MIB
        ),
    )(
        token_keys, resid_grad, kv_grad, kv_weight, editor_in, editor_bias.reshape(1, -1),
        editor_gain.reshape(1, -1), editor_out, prompt_len,
    )
    block = min(columns, 1024)
    tokens = keys_all.shape[0]
    return pl.pallas_call(
        update_kernel,
        grid=(columns // block,),
        out_shape=jax.ShapeDtypeStruct((key_columns, columns), BF16),
        in_specs=[
            smem,
            pl.BlockSpec((tokens, key_columns), lambda i: (0, 0)),
            pl.BlockSpec((tokens, block), lambda i: (0, i)),
        ],
        out_specs=pl.BlockSpec((key_columns, block), lambda i: (0, i)),
        compiler_params=pltpu.CompilerParams(vmem_limit_bytes=60 * MIB),
    )(prompt_len, keys_all, edited_all)


def solution(mesh):
    in_specs = (
        P("tp", "wide"),
        P("wide", "tp"),
        P("wide", "tp"),
        P("wide", "tp"),
        P("tp", None),
        P(),
        P("tp"),
        P(None, "tp"),
        P(),
    )
    out_specs = P("wide", "tp")
    return jax.shard_map(
        functools.partial(per_device, mesh.shape["tp"], mesh.shape["wide"]),
        mesh=mesh, in_specs=in_specs, out_specs=out_specs, check_vma=False,
    )
```
